32 devices in a mesh: dp: 2 (over core), seq: 16 (over z, y, x).
Axes of the slice: x: 2, y: 2, z: 4, core: 2. Of those that a mesh axis runs over, the one named last changes fastest.
Arguments:
- query: bfloat16 [2, 2048, 512], P('dp', 'seq'), may hold values from -6 to 6
- key_in: bfloat16 [2, 2048, 128], P('dp', 'seq'), may hold values from -4.5 to 4.5
- value_in: bfloat16 [2, 2048, 128], P('dp', 'seq'), may hold values from -6 to 6
- out_gain: float32 [512], replicated, may hold values from 0.1 to 1.9
- cotangent: bfloat16 [2, 2048, 512], P('dp', 'seq'), may hold values from -6 to 6
Outputs:
- attended: bfloat16 [2, 2048, 512], P('dp', 'seq')
- grad_query: bfloat16 [2, 2048, 512], P('dp', 'seq')
- grad_key: bfloat16 [2, 2048, 128], P('dp', 'seq')
- grad_value: bfloat16 [2, 2048, 128], P('dp', 'seq')
- grad_gain: float32 [512], replicated
The draws below stay inside these ranges and needn't reach their ends.
All inputs are finite; a program needn't handle non-finite values.
Results may differ from the reference program's by a relative error of at most 0.012.
The reference program's roundings to bfloat16 on the way count: a program that leaves them out, or rounds other values in their place, can miss the bound.
Values may be sent and summed in bfloat16 or wider, within the bound.
A program may use at most 128 MiB of HBM per device.

```python
import math
import jax
import jax.numpy as jnp
from jax import lax

HEADS = 4
KEY = 128
VAL = 128
LEN = 2048
BATCH = 2


def draw_key_in(key, part):
    noise_key = jax.random.fold_in(key, 202)
    keys_drawn = jnp.clip(jax.random.normal(noise_key, (BATCH, LEN, KEY), jnp.float32), -4.5, 4.5)
    return keys_drawn.astype(jnp.bfloat16)


def draw_query(key, part):
    noise_key = jax.random.fold_in(key, 303)
    queries = jnp.clip(2.5 * jax.random.normal(noise_key, (BATCH, LEN, HEADS * KEY), jnp.float32), -6.0, 6.0)
    return queries.astype(jnp.bfloat16)


def steps_of(own_key, shape, cuts, low, largest):
    level, own = 1.0, jax.random.fold_in(own_key, 6)
    for position, shards_of in cuts:
        draws = jnp.exp(jax.random.uniform(jax.random.fold_in(own, position), (shards_of,), jnp.float32, low / len(cuts), largest / len(cuts)))
        level = level * jnp.repeat(draws, shape[position] // shards_of).reshape([-1 if axis == position else 1 for axis in range(len(shape))])
    return level


def scatter_about(rng, extent, spread, most, cuts=(), kind=jnp.bfloat16):
    factor_of = steps_of(rng, extent, cuts, -0.22, 0.18) if cuts else 1.0
    values = jax.random.normal(rng, extent, jnp.float32) * spread * factor_of
    return jnp.minimum(jnp.maximum(values, -most), most).astype(kind)


def setup_inputs(seed: int = 0) -> dict:
    key_of = jax.random.split(jax.random.key(seed), 6)
    return {
        "query": draw_query(jax.random.fold_in(key_of[5], 71), 0),
        "key_in": draw_key_in(jax.random.fold_in(key_of[5], 71), 0),
        "value_in": scatter_about(key_of[2], (BATCH, LEN, VAL), 1.0, 6.0, ((0, 2), (1, 16))),
        "out_gain": jnp.clip(1.0 + 0.18 * jax.random.normal(key_of[3], (HEADS * VAL,), jnp.float32), 0.1, 1.9),
        "cotangent": scatter_about(key_of[4], (BATCH, LEN, HEADS * VAL), 1.0, 6.0, ((0, 2), (1, 16))),
    }


HIGHEST_PREC = lax.Precision.HIGHEST

def one_sequence(query, key_in, value_in, cotangent, out_gain):
    length = key_in.shape[0]
    block_size = math.gcd(length, 512)
    block_count = length // block_size
    score_scale = 1.0 / math.sqrt(KEY)
    key_f32 = key_in.astype(jnp.float32)
    value_f32 = value_in.astype(jnp.float32)
    gain_grid = out_gain.reshape(HEADS, VAL)
    query_blocks = query.reshape(block_count, block_size, HEADS, KEY)
    cotan_blocks = cotangent.reshape(block_count, block_size, HEADS, VAL)

    def advance(carry, block_pair):
        key_acc, value_acc, gain_acc = carry
        query_blk, cotan_blk = block_pair
        query_f32 = query_blk.astype(jnp.float32)
        scores = jnp.einsum('qhd,kd->hqk', query_f32, key_f32, precision=HIGHEST_PREC) * score_scale
        row_top = lax.optimization_barrier(jnp.max(scores, axis=2, keepdims=True))
        expo_rows = jnp.exp(scores - row_top)
        weights = lax.optimization_barrier((expo_rows / lax.optimization_barrier(jnp.sum(expo_rows, axis=2, keepdims=True))).astype(jnp.bfloat16))
        weight_f32 = weights.astype(jnp.float32)
        out_rows = jnp.einsum('hqk,kv->qhv', weight_f32, value_f32, precision=HIGHEST_PREC)
        attended = (out_rows * gain_grid).astype(jnp.bfloat16)
        upstream = cotan_blk.astype(jnp.float32)
        gain_acc = gain_acc + lax.optimization_barrier(jnp.sum(upstream * out_rows, axis=0))
        grad_out = lax.optimization_barrier((upstream * gain_grid).astype(jnp.bfloat16))
        grad_out_f32 = grad_out.astype(jnp.float32)
        delta_rows = lax.optimization_barrier(jnp.sum(grad_out_f32 * out_rows, axis=2))
        d_prob = jnp.einsum('qhv,kv->hqk', grad_out_f32, value_f32, precision=HIGHEST_PREC)
        d_score = lax.optimization_barrier((weight_f32 * (d_prob - delta_rows.T[:, :, None])).astype(jnp.bfloat16))
        score_grad_f32 = d_score.astype(jnp.float32)
        query_grad = (jnp.einsum('hqk,kd->qhd', score_grad_f32, key_f32, precision=HIGHEST_PREC) * score_scale).astype(jnp.bfloat16)
        key_acc = key_acc + jnp.einsum('hqk,qhd->kd', score_grad_f32, query_f32, precision=HIGHEST_PREC) * score_scale
        value_acc = value_acc + jnp.einsum('hqk,qhv->kv', weight_f32, grad_out_f32, precision=HIGHEST_PREC)
        return ((key_acc, value_acc, gain_acc), (attended.reshape(block_size, HEADS * VAL), query_grad.reshape(block_size, HEADS * KEY)))
    start_carry = (jnp.zeros((length, KEY), jnp.float32), jnp.zeros((length, VAL), jnp.float32), jnp.zeros((HEADS, VAL), jnp.float32))
    final_carry, outputs = lax.scan(advance, start_carry, (query_blocks, cotan_blocks))
    key_acc, value_acc, gain_acc = final_carry
    attended = outputs[0].reshape(length, HEADS * VAL)
    grad_query = outputs[1].reshape(length, HEADS * KEY)
    return (attended, grad_query, key_acc.astype(jnp.bfloat16), value_acc.astype(jnp.bfloat16), gain_acc.reshape(HEADS * VAL))

def reference(query, key_in, value_in, out_gain, cotangent):

    def per_sequence(items):
        return one_sequence(items[0], items[1], items[2], items[3], out_gain)
    attended, grad_query, grad_key, grad_value, gain_terms = lax.map(per_sequence, (query, key_in, value_in, cotangent))
    token_total = query.shape[0] * query.shape[1]
    grad_gain = lax.optimization_barrier(jnp.sum(gain_terms, axis=0)) / math.sqrt(token_total)
    return (attended, grad_query, grad_key, grad_value, grad_gain)
```

```python
import math

import jax
import jax.numpy as jnp
from jax import lax
from jax.experimental import pallas as pl
from jax.experimental.pallas import tpu as pltpu
from jax.sharding import PartitionSpec as P

HEADS = 4
KEY = 128
VAL = 128


def to_rows(tokens, heads):
    positions = tokens.shape[0]
    width = tokens.shape[1] // heads
    return (
        tokens.reshape(positions, heads, width).transpose(1, 0, 2).reshape(heads * positions, width)
    )


def to_tokens(rows_in, heads):
    positions = rows_in.shape[0] // heads
    width = rows_in.shape[1]
    return (
        rows_in.reshape(heads, positions, width)
        .transpose(1, 0, 2)
        .reshape(positions, heads * width)
    )


def contract_first(left_mat, right_mat):
    return lax.dot_general(
        left_mat, right_mat, (((0,), (0,)), ((), ())), preferred_element_type=jnp.float32
    )


def contract_last(left_mat, right_mat):
    return lax.dot_general(
        left_mat, right_mat, (((1,), (1,)), ((), ())), preferred_element_type=jnp.float32
    )


def body(query, key_in, value_in, out_gain, cotangent):
    keys_all, values_all = (
        lax.all_gather(key_in, "seq", axis=1, tiled=True),
        lax.all_gather(value_in, "seq", axis=1, tiled=True),
    )
    key_mat = keys_all[0]
    value_mat = values_all[0]
    length = key_mat.shape[0]
    positions = query.shape[1]
    shards = lax.axis_size("seq")
    score_scale = 1.0 / math.sqrt(KEY)
    query_rows = to_rows(query[0], HEADS)
    scores = contract_last(query_rows, key_mat) * score_scale
    row_top = jnp.max(scores, axis=1, keepdims=True)
    expo_rows = jnp.exp(scores - row_top)
    weights = (expo_rows / jnp.sum(expo_rows, axis=1, keepdims=True)).astype(jnp.bfloat16)
    out_rows = jnp.dot(weights, value_mat, preferred_element_type=jnp.float32)
    out_tokens = to_tokens(out_rows, HEADS)
    attended = (out_tokens * out_gain).astype(jnp.bfloat16)
    upstream = cotangent[0].astype(jnp.float32)
    gain_total = lax.psum(jnp.sum(upstream * out_tokens, axis=0), ("dp", "seq"))
    token_total = lax.axis_size("dp") * shards * positions
    grad_gain = gain_total / math.sqrt(token_total)
    grad_out = (upstream * out_gain).astype(jnp.bfloat16)
    grad_rows = to_rows(grad_out, HEADS)
    delta_rows = jnp.sum(grad_rows.astype(jnp.float32) * out_rows, axis=1, keepdims=True)
    block_size = 2048
    block_starts = jnp.arange(length // block_size, dtype=jnp.int32) * block_size
    query_zero = jnp.zeros((query_rows.shape[0], KEY), jnp.float32)

    def score_grad(offset_at):
        key_part = lax.dynamic_slice_in_dim(key_mat, offset_at, block_size, 0)
        value_part = lax.dynamic_slice_in_dim(value_mat, offset_at, block_size, 0)
        weight_part = lax.dynamic_slice_in_dim(weights, offset_at, block_size, 1)
        d_prob = contract_last(grad_rows, value_part)
        d_score = (weight_part.astype(jnp.float32) * (d_prob - delta_rows)).astype(jnp.bfloat16)
        return (d_score, key_part, weight_part)

    def advance_both(query_acc, offset_at):
        d_score, key_part, weight_part = score_grad(offset_at)
        query_acc = query_acc + jnp.dot(d_score, key_part, preferred_element_type=jnp.float32)
        key_term = contract_first(d_score, query_rows) * score_scale
        value_term = contract_first(weight_part, grad_rows)
        return (query_acc, (key_term, value_term))

    query_acc, both_terms = lax.scan(advance_both, query_zero, block_starts)
    key_recv, value_recv = (
        lax.all_to_all(
            both_terms[0].reshape(shards, positions, KEY),
            "seq",
            split_axis=0,
            concat_axis=0,
            tiled=True,
        ),
        lax.all_to_all(
            both_terms[1].reshape(shards, positions, VAL),
            "seq",
            split_axis=0,
            concat_axis=0,
            tiled=True,
        ),
    )
    grad_key = jnp.sum(key_recv, axis=0)
    grad_value = jnp.sum(value_recv, axis=0)
    grad_query = to_tokens(query_acc * score_scale, HEADS).astype(jnp.bfloat16)
    return (
        attended[None],
        grad_query[None],
        grad_key.astype(jnp.bfloat16)[None],
        grad_value.astype(jnp.bfloat16)[None],
        grad_gain,
    )


BF = jnp.bfloat16
F32 = jnp.float32
DEPTH = 4
SIDE = 2
SLOTS = DEPTH * SIDE * SIDE
COPIES = 80


def fused_kernel(
    q_ref, k_ref, v_ref, gain_ref, cot_ref,
    att_ref, gq_ref, gk_ref, gv_ref, gg_ref,
    kbuf, vbuf, qbuf, cbuf, qrows, grows, gtrans, ebuf, dpbuf, pbuf, dsbuf,
    ksend, vsend, kown, vown, kfirst, ksecond, kthird, vfirst, vsecond, vthird,
    gsend, grecv, local_sem, send_sem, recv_sem,
):
    dp = lax.axis_index("dp")
    me = lax.axis_index("seq")
    x = me % 2
    y = (me // 2) % 2
    z = me // 4
    other_core = (1 - dp, me)
    x_peer = (dp, me + 1 - 2 * x)
    y_peer = (dp, me + 2 - 4 * y)
    low = me % 4
    z_peers = {
        1: (dp, (z + 1 - 2 * (z % 2)) * 4 + low),
        2: (dp, ((z + 2) % 4) * 4 + low),
        3: (dp, (3 - z) * 4 + low),
    }

    def local(src, dst, index):
        copy = pltpu.make_async_copy(src, dst, local_sem.at[index])
        copy.start()
        return copy

    k_local = local(k_ref.at[0], kbuf.at[0], 0)
    v_local = local(v_ref.at[0], vbuf.at[0], 1)
    q_local = local(q_ref.at[0], qbuf, 2)
    c_local = local(cot_ref.at[0], cbuf, 3)

    barrier = pltpu.get_barrier_semaphore()
    peers = [other_core, x_peer, y_peer] + [z_peers[d] for d in (1, 2, 3)]
    for peer in peers:
        pl.semaphore_signal(barrier, inc=1, device_id=peer, device_id_type=pl.DeviceIdType.MESH)
    pl.semaphore_wait(barrier, len(peers))

    sent = []

    def send(src, dst, peer):
        index = len(sent)
        copy = pltpu.make_async_remote_copy(
            src_ref=src, dst_ref=dst, send_sem=send_sem.at[index], recv_sem=recv_sem.at[index],
            device_id=peer, device_id_type=pl.DeviceIdType.MESH,
        )
        copy.start()
        sent.append(copy)
        return copy

    k_in, v_in = {}, {}
    k_local.wait()
    for d in (1, 2, 3):
        k_in[4 * d] = send(kbuf.at[0], kbuf.at[4 * d], z_peers[d])
    k_in[1] = send(kbuf.at[0], kbuf.at[1], x_peer)
    v_local.wait()
    v_in[2] = send(vbuf.at[0], vbuf.at[2], y_peer)
    for d in (1, 2, 3):
        v_in[4 * d] = send(vbuf.at[0], vbuf.at[4 * d], z_peers[d])
    k_in[2] = send(kbuf.at[0], kbuf.at[2], y_peer)
    v_in[1] = send(vbuf.at[0], vbuf.at[1], x_peer)

    positions = qbuf.shape[0]
    gain = gain_ref[...]
    q_local.wait()
    c_local.wait()
    for h in range(HEADS):
        lanes = slice(h * KEY, (h + 1) * KEY)
        rows = slice(h * positions, (h + 1) * positions)
        qrows[rows, :] = qbuf[:, lanes]
        out_grad = (cbuf[:, lanes].astype(F32) * gain[:, lanes]).astype(BF)
        grows[rows, :] = out_grad
        gtrans[:, rows] = out_grad.astype(F32).T

    rate = math.log2(math.e) / math.sqrt(KEY)
    score_scale = 1.0 / math.sqrt(KEY)
    tops, sums = {}, {}

    def score(r):
        raw = contract_last(kbuf[r], qrows[...])
        top = jnp.max(raw, axis=0, keepdims=True)
        expo = jnp.exp2((raw - top) * rate)
        tops[r] = top
        sums[r] = jnp.sum(expo, axis=0, keepdims=True)
        ebuf[r] = expo

    def d_prob(r):
        dpbuf[r] = contract_last(vbuf[r], grows[...])

    score(0)
    d_prob(0)
    for d in range(4):
        base = 4 * d
        if d:
            k_in[base].wait_recv()
            k_in[base + 1] = send(kbuf.at[base], kbuf.at[base + 1], x_peer)
            k_in[base + 2] = send(kbuf.at[base], kbuf.at[base + 2], y_peer)
            v_in[base].wait_recv()
            v_in[base + 2] = send(vbuf.at[base], vbuf.at[base + 2], y_peer)
            v_in[base + 1] = send(vbuf.at[base], vbuf.at[base + 1], x_peer)
            score(base)
            d_prob(base)
        if d != 1:
            done = [0] if d == 0 else [d - 1] if d > 2 else [1]
            for e in done:
                at = 4 * e
                k_in[at + 1].wait_recv()
                k_in[at + 3] = send(kbuf.at[at + 1], kbuf.at[at + 3], y_peer)
                v_in[at + 2].wait_recv()
                v_in[at + 3] = send(vbuf.at[at + 2], vbuf.at[at + 3], x_peer)
                score(at + 1)
                d_prob(at + 2)
    k_in[13].wait_recv()
    k_in[15] = send(kbuf.at[13], kbuf.at[15], y_peer)
    v_in[14].wait_recv()
    v_in[15] = send(vbuf.at[14], vbuf.at[15], x_peer)
    score(13)
    d_prob(14)
    for d in range(4):
        k_in[4 * d + 2].wait_recv()
        score(4 * d + 2)
        v_in[4 * d + 1].wait_recv()
        d_prob(4 * d + 1)
    for d in range(4):
        k_in[4 * d + 3].wait_recv()
        score(4 * d + 3)
        v_in[4 * d + 3].wait_recv()
        d_prob(4 * d + 3)

    top_all = tops[0]
    for r in range(1, SLOTS):
        top_all = jnp.maximum(top_all, tops[r])
    factors = [jnp.exp2((tops[r] - top_all) * rate) for r in range(SLOTS)]
    total = sums[0] * factors[0]
    for r in range(1, SLOTS):
        total = total + sums[r] * factors[r]
    inverse = 1.0 / total
    out_t = None
    for r in range(SLOTS):
        weight = (ebuf[r] * (factors[r] * inverse)).astype(BF)
        pbuf[r] = weight
        term = jnp.dot(vbuf[r].T, weight, preferred_element_type=F32)
        out_t = term if out_t is None else out_t + term
    delta = jnp.sum(gtrans[...] * out_t, axis=0, keepdims=True)

    k_first, k_second, k_third, v_first, v_second, v_third = {}, {}, {}, {}, {}, {}

    def terms(r):
        weight = pbuf[r]
        d_score = (weight.astype(F32) * (dpbuf[r] - delta)).astype(BF)
        dsbuf[r] = d_score
        key_term = jnp.dot(d_score, qrows[...], preferred_element_type=F32) * score_scale
        value_term = jnp.dot(weight, grows[...], preferred_element_type=F32)
        return key_term, value_term

    for d in (3, 2, 1, 0):
        r = 4 * d + 3
        key_term, value_term = terms(r)
        ksend[r] = key_term.astype(BF)
        vsend[r] = value_term.astype(BF)
        k_first[d, 1] = send(ksend.at[r], kfirst.at[2 * d + 1], y_peer)
        v_first[d, 1] = send(vsend.at[r], vfirst.at[2 * d + 1], x_peer)
    for d in (3, 2, 1, 0):
        r = 4 * d + 2
        key_term, value_term = terms(r)
        ksend[r] = key_term.astype(BF)
        k_first[d, 0] = send(ksend.at[r], kfirst.at[2 * d], y_peer)
        vown[2 * d + 1] = value_term
        r = 4 * d + 1
        key_term, value_term = terms(r)
        vsend[r] = value_term.astype(BF)
        v_first[d, 0] = send(vsend.at[r], vfirst.at[2 * d], x_peer)
        kown[2 * d + 1] = key_term

    gain_terms = []
    for h in range(HEADS):
        lanes = slice(h * VAL, (h + 1) * VAL)
        out_h = out_t[:, h * positions : (h + 1) * positions].T
        att_ref[0, :, lanes] = (out_h * gain[:, lanes]).astype(BF)
        gain_terms.append(jnp.sum(cbuf[:, lanes].astype(F32) * out_h, axis=0, keepdims=True))
    gain_sum = jnp.broadcast_to(jnp.concatenate(gain_terms, axis=1), (8, HEADS * VAL))
    gsend[0] = gain_sum
    gain_copy = send(gsend.at[0], grecv.at[0], other_core)

    for d in (3, 2, 1, 0):
        k_first[d, 1].wait_recv()
        ksend[4 * d + 1] = (kown[2 * d + 1] + kfirst[2 * d + 1].astype(F32)).astype(BF)
        k_second[d] = send(ksend.at[4 * d + 1], ksecond.at[d], x_peer)
        v_first[d, 1].wait_recv()
        vsend[4 * d + 2] = (vown[2 * d + 1] + vfirst[2 * d + 1].astype(F32)).astype(BF)
        v_second[d] = send(vsend.at[4 * d + 2], vsecond.at[d], y_peer)

    gain_copy.wait_recv()
    gain_sum = gain_sum + grecv[0]
    gsend[1] = gain_sum
    gain_copy = send(gsend.at[1], grecv.at[1], x_peer)

    for d in (3, 2, 1, 0):
        key_term, value_term = terms(4 * d)
        kown[2 * d] = key_term
        vown[2 * d] = value_term

    gain_copy.wait_recv()
    gain_sum = gain_sum + grecv[1]
    gsend[2] = gain_sum
    gain_copy = send(gsend.at[2], grecv.at[2], y_peer)

    query_t = None
    for r in range(SLOTS):
        term = jnp.dot(kbuf[r].T, dsbuf[r], preferred_element_type=F32)
        query_t = term if query_t is None else query_t + term
    for h in range(HEADS):
        part = query_t[:, h * positions : (h + 1) * positions] * score_scale
        gq_ref[0, :, h * KEY : (h + 1) * KEY] = part.T.astype(BF)

    gain_copy.wait_recv()
    gain_sum = gain_sum + grecv[2]
    gsend[3] = gain_sum
    gain_copies = [send(gsend.at[3], grecv.at[2 + d], z_peers[d]) for d in (1, 2, 3)]

    for d in (3, 2, 1, 0):
        k_first[d, 0].wait_recv()
        k_second[d].wait_recv()
        key_sum = kown[2 * d] + kfirst[2 * d].astype(F32) + ksecond[d].astype(F32)
        v_first[d, 0].wait_recv()
        v_second[d].wait_recv()
        value_sum = vown[2 * d] + vfirst[2 * d].astype(F32) + vsecond[d].astype(F32)
        if d:
            ksend[4 * d] = key_sum.astype(BF)
            k_third[d] = send(ksend.at[4 * d], kthird.at[d - 1], z_peers[d])
            vsend[4 * d] = value_sum.astype(BF)
            v_third[d] = send(vsend.at[4 * d], vthird.at[d - 1], z_peers[d])

    for copy in gain_copies:
        copy.wait_recv()
    gain_sum = (gain_sum + grecv[3]) + (grecv[4] + grecv[5])
    token_total = lax.axis_size("dp") * lax.axis_size("seq") * positions
    gg_ref[...] = gain_sum[0:1, :] / math.sqrt(token_total)

    for d in (3, 2, 1):
        k_third[d].wait_recv()
        key_sum = key_sum + kthird[d - 1].astype(F32)
        v_third[d].wait_recv()
        value_sum = value_sum + vthird[d - 1].astype(F32)
    gk_ref[0] = key_sum.astype(BF)
    gv_ref[0] = value_sum.astype(BF)
    for copy in sent:
        copy.wait_send()


def fused_body(query, key_in, value_in, out_gain, cotangent):
    positions = query.shape[1]
    rows = HEADS * positions
    any_space = pl.BlockSpec(memory_space=pl.ANY)
    vmem = pl.BlockSpec(memory_space=pltpu.VMEM)
    key_slot = lambda count, kind: pltpu.VMEM((count, positions, KEY), kind)
    scratch = [
        key_slot(SLOTS, BF), key_slot(SLOTS, BF),
        pltpu.VMEM((positions, HEADS * KEY), BF), pltpu.VMEM((positions, HEADS * VAL), BF),
        pltpu.VMEM((rows, KEY), BF), pltpu.VMEM((rows, VAL), BF), pltpu.VMEM((VAL, rows), F32),
        pltpu.VMEM((SLOTS, positions, rows), F32), pltpu.VMEM((SLOTS, positions, rows), F32),
        pltpu.VMEM((SLOTS, positions, rows), BF), pltpu.VMEM((SLOTS, positions, rows), BF),
        key_slot(SLOTS, BF), key_slot(SLOTS, BF),
        key_slot(8, F32), key_slot(8, F32),
        key_slot(8, BF), key_slot(4, BF), key_slot(3, BF),
        key_slot(8, BF), key_slot(4, BF), key_slot(3, BF),
        pltpu.VMEM((4, 8, HEADS * VAL), F32), pltpu.VMEM((6, 8, HEADS * VAL), F32),
        pltpu.SemaphoreType.DMA((4,)), pltpu.SemaphoreType.DMA((COPIES,)), pltpu.SemaphoreType.DMA((COPIES,)),
    ]
    outs = pl.pallas_call(
        fused_kernel,
        out_shape=[
            jax.ShapeDtypeStruct(query.shape, BF),
            jax.ShapeDtypeStruct(query.shape, BF),
            jax.ShapeDtypeStruct(key_in.shape, BF),
            jax.ShapeDtypeStruct(value_in.shape, BF),
            jax.ShapeDtypeStruct((1, HEADS * VAL), F32),
        ],
        in_specs=[any_space, any_space, any_space, vmem, any_space],
        out_specs=[vmem] * 5,
        scratch_shapes=scratch,
        compiler_params=pltpu.CompilerParams(
            collective_id=0, has_side_effects=True, vmem_limit_bytes=48 * 1024 * 1024
        ),
        cost_estimate=pl.CostEstimate(
            flops=12 * rows * SLOTS * positions * KEY,
            bytes_accessed=8 * positions * HEADS * KEY,
            transcendentals=rows * SLOTS * positions,
        ),
    )(query, key_in, value_in, out_gain.reshape(1, -1), cotangent)
    return (*outs[:4], outs[4].reshape(-1))


def solution(mesh):
    placed = (
        P("dp", "seq", None),
        P("dp", "seq", None),
        P("dp", "seq", None),
        P(),
        P("dp", "seq", None),
    )
    fits = mesh.shape["seq"] == SLOTS and mesh.shape["dp"] == 2
    return jax.shard_map(
        fused_body if fits else body,
        mesh=mesh,
        in_specs=placed,
        out_specs=(
            P("dp", "seq", None),
            P("dp", "seq", None),
            P("dp", "seq", None),
            P("dp", "seq", None),
            P(),
        ),
        check_vma=False,
    )
```

```python
import math

import jax
import jax.numpy as jnp
from jax import lax
from jax.experimental import pallas as pl
from jax.experimental.pallas import tpu as pltpu
from jax.sharding import PartitionSpec as P

HEADS = 4
KEY = 128
VAL = 128


def to_rows(tokens, heads):
    positions = tokens.shape[0]
    width = tokens.shape[1] // heads
    return (
        tokens.reshape(positions, heads, width).transpose(1, 0, 2).reshape(heads * positions, width)
    )


def to_tokens(rows_in, heads):
    positions = rows_in.shape[0] // heads
    width = rows_in.shape[1]
    return (
        rows_in.reshape(heads, positions, width)
        .transpose(1, 0, 2)
        .reshape(positions, heads * width)
    )


def contract_first(left_mat, right_mat):
    return lax.dot_general(
        left_mat, right_mat, (((0,), (0,)), ((), ())), preferred_element_type=jnp.float32
    )


def contract_last(left_mat, right_mat):
    return lax.dot_general(
        left_mat, right_mat, (((1,), (1,)), ((), ())), preferred_element_type=jnp.float32
    )


def body(query, key_in, value_in, out_gain, cotangent):
    keys_all, values_all = (
        lax.all_gather(key_in, "seq", axis=1, tiled=True),
        lax.all_gather(value_in, "seq", axis=1, tiled=True),
    )
    key_mat = keys_all[0]
    value_mat = values_all[0]
    length = key_mat.shape[0]
    positions = query.shape[1]
    shards = lax.axis_size("seq")
    score_scale = 1.0 / math.sqrt(KEY)
    query_rows = to_rows(query[0], HEADS)
    scores = contract_last(query_rows, key_mat) * score_scale
    row_top = jnp.max(scores, axis=1, keepdims=True)
    expo_rows = jnp.exp(scores - row_top)
    weights = (expo_rows / jnp.sum(expo_rows, axis=1, keepdims=True)).astype(jnp.bfloat16)
    out_rows = jnp.dot(weights, value_mat, preferred_element_type=jnp.float32)
    out_tokens = to_tokens(out_rows, HEADS)
    attended = (out_tokens * out_gain).astype(jnp.bfloat16)
    upstream = cotangent[0].astype(jnp.float32)
    gain_total = lax.psum(jnp.sum(upstream * out_tokens, axis=0), ("dp", "seq"))
    token_total = lax.axis_size("dp") * shards * positions
    grad_gain = gain_total / math.sqrt(token_total)
    grad_out = (upstream * out_gain).astype(jnp.bfloat16)
    grad_rows = to_rows(grad_out, HEADS)
    delta_rows = jnp.sum(grad_rows.astype(jnp.float32) * out_rows, axis=1, keepdims=True)
    block_size = 2048
    block_starts = jnp.arange(length // block_size, dtype=jnp.int32) * block_size
    query_zero = jnp.zeros((query_rows.shape[0], KEY), jnp.float32)

    def score_grad(offset_at):
        key_part = lax.dynamic_slice_in_dim(key_mat, offset_at, block_size, 0)
        value_part = lax.dynamic_slice_in_dim(value_mat, offset_at, block_size, 0)
        weight_part = lax.dynamic_slice_in_dim(weights, offset_at, block_size, 1)
        d_prob = contract_last(grad_rows, value_part)
        d_score = (weight_part.astype(jnp.float32) * (d_prob - delta_rows)).astype(jnp.bfloat16)
        return (d_score, key_part, weight_part)

    def advance_both(query_acc, offset_at):
        d_score, key_part, weight_part = score_grad(offset_at)
        query_acc = query_acc + jnp.dot(d_score, key_part, preferred_element_type=jnp.float32)
        key_term = contract_first(d_score, query_rows) * score_scale
        value_term = contract_first(weight_part, grad_rows)
        return (query_acc, (key_term, value_term))

    query_acc, both_terms = lax.scan(advance_both, query_zero, block_starts)
    key_recv, value_recv = (
        lax.all_to_all(
            both_terms[0].reshape(shards, positions, KEY),
            "seq",
            split_axis=0,
            concat_axis=0,
            tiled=True,
        ),
        lax.all_to_all(
            both_terms[1].reshape(shards, positions, VAL),
            "seq",
            split_axis=0,
            concat_axis=0,
            tiled=True,
        ),
    )
    grad_key = jnp.sum(key_recv, axis=0)
    grad_value = jnp.sum(value_recv, axis=0)
    grad_query = to_tokens(query_acc * score_scale, HEADS).astype(jnp.bfloat16)
    return (
        attended[None],
        grad_query[None],
        grad_key.astype(jnp.bfloat16)[None],
        grad_value.astype(jnp.bfloat16)[None],
        grad_gain,
    )


BF = jnp.bfloat16
F32 = jnp.float32
DEPTH = 4
SIDE = 2
SLOTS = DEPTH * SIDE * SIDE
COPIES = 80
VMEM_BYTES = 60 * 1024 * 1024


def fused_kernel(
    q_ref, k_ref, v_ref, gain_ref, cot_ref,
    att_ref, gq_ref, gk_ref, gv_ref, gg_ref,
    kbuf, vbuf, qbuf, cbuf, qrows, grows, gtrans, ebuf, dpbuf, pbuf, dsbuf,
    ksend, vsend, kown, vown, kfirst, ksecond, kthird, vfirst, vsecond, vthird,
    gsend, grecv, abuf, qout, local_sem, send_sem, recv_sem,
):
    dp = lax.axis_index("dp")
    me = lax.axis_index("seq")
    x = me % 2
    y = (me // 2) % 2
    z = me // 4
    other_core = (1 - dp, me)
    x_peer = (dp, me + 1 - 2 * x)
    y_peer = (dp, me + 2 - 4 * y)
    low = me % 4
    z_peers = {
        1: (dp, (z + 1 - 2 * (z % 2)) * 4 + low),
        2: (dp, ((z + 2) % 4) * 4 + low),
        3: (dp, (3 - z) * 4 + low),
    }

    def local(src, dst, index):
        copy = pltpu.make_async_copy(src, dst, local_sem.at[index])
        copy.start()
        return copy

    k_local = local(k_ref.at[0], kbuf.at[0], 0)
    v_local = local(v_ref.at[0], vbuf.at[0], 1)
    q_local = local(q_ref.at[0], qbuf, 2)
    c_local = local(cot_ref.at[0], cbuf, 3)

    barrier = pltpu.get_barrier_semaphore()
    peers = [other_core, x_peer, y_peer] + [z_peers[d] for d in (1, 2, 3)]
    for peer in peers:
        pl.semaphore_signal(barrier, inc=1, device_id=peer, device_id_type=pl.DeviceIdType.MESH)
    pl.semaphore_wait(barrier, len(peers))

    sent = []

    def send(src, dst, peer):
        index = len(sent)
        copy = pltpu.make_async_remote_copy(
            src_ref=src, dst_ref=dst, send_sem=send_sem.at[index], recv_sem=recv_sem.at[index],
            device_id=peer, device_id_type=pl.DeviceIdType.MESH,
        )
        copy.start()
        sent.append(copy)
        return copy

    k_in, v_in = {}, {}
    k_local.wait()
    v_local.wait()
    for d in (1, 2, 3):
        k_in[4 * d] = send(kbuf.at[0], kbuf.at[4 * d], z_peers[d])
        v_in[4 * d] = send(vbuf.at[0], vbuf.at[4 * d], z_peers[d])
        if d == 1:
            k_in[1] = send(kbuf.at[0], kbuf.at[1], x_peer)
            v_in[2] = send(vbuf.at[0], vbuf.at[2], y_peer)
    k_in[2] = send(kbuf.at[0], kbuf.at[2], y_peer)
    v_in[1] = send(vbuf.at[0], vbuf.at[1], x_peer)

    positions = qbuf.shape[0]
    gain = gain_ref[...]
    q_local.wait()
    c_local.wait()
    for h in range(HEADS):
        lanes = slice(h * KEY, (h + 1) * KEY)
        rows = slice(h * positions, (h + 1) * positions)
        qrows[rows, :] = qbuf[:, lanes]
        out_grad = (cbuf[:, lanes].astype(F32) * gain[:, lanes]).astype(BF)
        grows[rows, :] = out_grad
        gtrans[:, rows] = out_grad.astype(F32).T

    rate = math.log2(math.e) / math.sqrt(KEY)
    score_scale = 1.0 / math.sqrt(KEY)
    tops, sums = {}, {}

    def score(r):
        raw = contract_last(kbuf[r], qrows[...])
        top = jnp.max(raw, axis=0, keepdims=True)
        expo = jnp.exp2((raw - top) * rate)
        tops[r] = top
        sums[r] = jnp.sum(expo, axis=0, keepdims=True)
        ebuf[r] = expo

    def d_prob(r):
        dpbuf[r] = contract_last(vbuf[r], grows[...])

    score(0)
    d_prob(0)
    for d in range(4):
        base = 4 * d
        if d:
            k_in[base].wait_recv()
            k_in[base + 1] = send(kbuf.at[base], kbuf.at[base + 1], x_peer)
            k_in[base + 2] = send(kbuf.at[base], kbuf.at[base + 2], y_peer)
            v_in[base].wait_recv()
            v_in[base + 2] = send(vbuf.at[base], vbuf.at[base + 2], y_peer)
            v_in[base + 1] = send(vbuf.at[base], vbuf.at[base + 1], x_peer)
            score(base)
            d_prob(base)
        if d != 1:
            done = [0] if d == 0 else [d - 1] if d > 2 else [1]
            for e in done:
                at = 4 * e
                k_in[at + 1].wait_recv()
                k_in[at + 3] = send(kbuf.at[at + 1], kbuf.at[at + 3], y_peer)
                v_in[at + 2].wait_recv()
                v_in[at + 3] = send(vbuf.at[at + 2], vbuf.at[at + 3], x_peer)
                score(at + 1)
                d_prob(at + 2)
    k_in[13].wait_recv()
    k_in[15] = send(kbuf.at[13], kbuf.at[15], y_peer)
    v_in[14].wait_recv()
    v_in[15] = send(vbuf.at[14], vbuf.at[15], x_peer)
    score(13)
    d_prob(14)
    for d in range(4):
        k_in[4 * d + 2].wait_recv()
        score(4 * d + 2)
        v_in[4 * d + 1].wait_recv()
        d_prob(4 * d + 1)
    for d in range(4):
        k_in[4 * d + 3].wait_recv()
        score(4 * d + 3)
        v_in[4 * d + 3].wait_recv()
        d_prob(4 * d + 3)

    top_all = tops[0]
    for r in range(1, SLOTS):
        top_all = jnp.maximum(top_all, tops[r])
    factors = [jnp.exp2((tops[r] - top_all) * rate) for r in range(SLOTS)]
    total = sums[0] * factors[0]
    for r in range(1, SLOTS):
        total = total + sums[r] * factors[r]
    inverse = 1.0 / total
    out_t = None
    for r in range(SLOTS):
        weight = (ebuf[r] * (factors[r] * inverse)).astype(BF)
        pbuf[r] = weight
        term = jnp.dot(vbuf[r].T, weight, preferred_element_type=F32)
        out_t = term if out_t is None else out_t + term
    delta = jnp.sum(gtrans[...] * out_t, axis=0, keepdims=True)

    gain_terms = []
    for h in range(HEADS):
        lanes = slice(h * VAL, (h + 1) * VAL)
        out_h = out_t[:, h * positions : (h + 1) * positions].T
        abuf[:, lanes] = (out_h * gain[:, lanes]).astype(BF)
        gain_terms.append(jnp.sum(cbuf[:, lanes].astype(F32) * out_h, axis=0, keepdims=True))
    gain_sum = jnp.concatenate(gain_terms, axis=1)
    gsend[0] = gain_sum
    gain_copy = send(gsend.at[0], grecv.at[0], other_core)
    att_out = local(abuf, att_ref.at[0], 4)

    k_first, k_second, k_third, v_first, v_second, v_third = {}, {}, {}, {}, {}, {}

    def terms(r):
        weight = pbuf[r]
        d_score = (weight.astype(F32) * (dpbuf[r] - delta)).astype(BF)
        dsbuf[r] = d_score
        key_term = jnp.dot(d_score, qrows[...], preferred_element_type=F32) * score_scale
        value_term = jnp.dot(weight, grows[...], preferred_element_type=F32)
        return key_term, value_term

    def first_stage(d):
        r = 4 * d + 3
        key_term, value_term = terms(r)
        ksend[r] = key_term.astype(BF)
        k_first[d, 1] = send(ksend.at[r], kfirst.at[2 * d + 1], y_peer)
        vsend[r] = value_term.astype(BF)
        v_first[d, 1] = send(vsend.at[r], vfirst.at[2 * d + 1], x_peer)
        r = 4 * d + 2
        key_term, value_term = terms(r)
        ksend[r] = key_term.astype(BF)
        k_first[d, 0] = send(ksend.at[r], kfirst.at[2 * d], y_peer)
        vown[2 * d + 1] = value_term
        r = 4 * d + 1
        key_term, value_term = terms(r)
        vsend[r] = value_term.astype(BF)
        v_first[d, 0] = send(vsend.at[r], vfirst.at[2 * d], x_peer)
        kown[2 * d + 1] = key_term
        key_term, value_term = terms(4 * d)
        kown[2 * d] = key_term
        vown[2 * d] = value_term

    def second_stage(d):
        k_first[d, 1].wait_recv()
        ksend[4 * d + 1] = (kown[2 * d + 1] + kfirst[2 * d + 1].astype(F32)).astype(BF)
        k_second[d] = send(ksend.at[4 * d + 1], ksecond.at[d], x_peer)
        v_first[d, 1].wait_recv()
        vsend[4 * d + 2] = (vown[2 * d + 1] + vfirst[2 * d + 1].astype(F32)).astype(BF)
        v_second[d] = send(vsend.at[4 * d + 2], vsecond.at[d], y_peer)

    def third_stage(d):
        k_first[d, 0].wait_recv()
        k_second[d].wait_recv()
        key_sum = kown[2 * d] + kfirst[2 * d].astype(F32) + ksecond[d].astype(F32)
        if d:
            ksend[4 * d] = key_sum.astype(BF)
            k_third[d] = send(ksend.at[4 * d], kthird.at[d - 1], z_peers[d])
        v_first[d, 0].wait_recv()
        v_second[d].wait_recv()
        value_sum = vown[2 * d] + vfirst[2 * d].astype(F32) + vsecond[d].astype(F32)
        if d:
            vsend[4 * d] = value_sum.astype(BF)
            v_third[d] = send(vsend.at[4 * d], vthird.at[d - 1], z_peers[d])
        return key_sum, value_sum

    first_stage(3)
    gain_copy.wait_recv()
    gain_sum = gain_sum + grecv[0]
    gsend[1] = gain_sum
    gain_copy = send(gsend.at[1], grecv.at[1], x_peer)
    first_stage(2)
    second_stage(3)
    first_stage(1)
    second_stage(2)
    third_stage(3)
    gain_copy.wait_recv()
    gain_sum = gain_sum + grecv[1]
    gsend[2] = gain_sum
    gain_copy = send(gsend.at[2], grecv.at[2], y_peer)
    first_stage(0)
    second_stage(1)
    third_stage(2)
    second_stage(0)
    third_stage(1)
    gain_copy.wait_recv()
    gain_sum = gain_sum + grecv[2]
    gsend[3] = gain_sum
    gain_copies = [send(gsend.at[3], grecv.at[2 + d], z_peers[d]) for d in (1, 2, 3)]

    query_t = None
    for r in range(SLOTS):
        term = jnp.dot(kbuf[r].T, dsbuf[r], preferred_element_type=F32)
        query_t = term if query_t is None else query_t + term
    for h in range(HEADS):
        part = query_t[:, h * positions : (h + 1) * positions] * score_scale
        qout[:, h * KEY : (h + 1) * KEY] = part.T.astype(BF)
    q_out = local(qout, gq_ref.at[0], 5)

    key_sum, value_sum = third_stage(0)
    for d in (3, 2, 1):
        k_third[d].wait_recv()
        key_sum = key_sum + kthird[d - 1].astype(F32)
        v_third[d].wait_recv()
        value_sum = value_sum + vthird[d - 1].astype(F32)
    gk_ref[0] = key_sum.astype(BF)
    gv_ref[0] = value_sum.astype(BF)
    for copy in gain_copies:
        copy.wait_recv()
    gain_sum = (gain_sum + grecv[3]) + (grecv[4] + grecv[5])
    token_total = lax.axis_size("dp") * lax.axis_size("seq") * positions
    gg_ref[...] = gain_sum / math.sqrt(token_total)
    att_out.wait()
    q_out.wait()
    for copy in sent:
        copy.wait_send()


def hand_over(*refs):
    sources, targets, held = refs[:5], refs[5:10], refs[10:15]
    in_sem, out_sem = refs[15:]
    reads = [pltpu.make_async_copy(sources[i], held[i], in_sem.at[i]) for i in range(5)]
    writes = [pltpu.make_async_copy(held[i], targets[i], out_sem.at[i]) for i in range(5)]
    for copy in reads:
        copy.start()
    for read, write in zip(reads, writes):
        read.wait()
        write.start()
    for copy in writes:
        copy.wait()


def fused_body(query, key_in, value_in, out_gain, cotangent):
    positions = query.shape[1]
    rows = HEADS * positions
    any_space = pl.BlockSpec(memory_space=pl.ANY)
    vmem = pl.BlockSpec(memory_space=pltpu.VMEM)
    key_slot = lambda count, kind: pltpu.VMEM((count, positions, KEY), kind)
    scratch = [
        key_slot(SLOTS, BF), key_slot(SLOTS, BF),
        pltpu.VMEM((positions, HEADS * KEY), BF), pltpu.VMEM((positions, HEADS * VAL), BF),
        pltpu.VMEM((rows, KEY), BF), pltpu.VMEM((rows, VAL), BF), pltpu.VMEM((VAL, rows), F32),
        pltpu.VMEM((SLOTS, positions, rows), F32), pltpu.VMEM((SLOTS, positions, rows), F32),
        pltpu.VMEM((SLOTS, positions, rows), BF), pltpu.VMEM((SLOTS, positions, rows), BF),
        key_slot(SLOTS, BF), key_slot(SLOTS, BF),
        key_slot(8, F32), key_slot(8, F32),
        key_slot(8, BF), key_slot(4, BF), key_slot(3, BF),
        key_slot(8, BF), key_slot(4, BF), key_slot(3, BF),
        pltpu.VMEM((4, 1, HEADS * VAL), F32), pltpu.VMEM((6, 1, HEADS * VAL), F32),
        pltpu.VMEM((positions, HEADS * VAL), BF), pltpu.VMEM((positions, HEADS * KEY), BF),
        pltpu.SemaphoreType.DMA((6,)), pltpu.SemaphoreType.DMA((COPIES,)), pltpu.SemaphoreType.DMA((COPIES,)),
    ]
    outs = pl.pallas_call(
        fused_kernel,
        out_shape=[
            jax.ShapeDtypeStruct(query.shape, BF),
            jax.ShapeDtypeStruct(query.shape, BF),
            jax.ShapeDtypeStruct(key_in.shape, BF),
            jax.ShapeDtypeStruct(value_in.shape, BF),
            jax.ShapeDtypeStruct((1, HEADS * VAL), F32),
        ],
        in_specs=[any_space, any_space, any_space, vmem, any_space],
        out_specs=[any_space, any_space, vmem, vmem, vmem],
        scratch_shapes=scratch,
        compiler_params=pltpu.CompilerParams(
            collective_id=0, has_side_effects=True, vmem_limit_bytes=VMEM_BYTES
        ),
        cost_estimate=pl.CostEstimate(
            flops=12 * rows * SLOTS * positions * KEY,
            bytes_accessed=8 * positions * HEADS * KEY,
            transcendentals=rows * SLOTS * positions,
        ),
    )(query, key_in, value_in, out_gain.reshape(1, -1), cotangent)
    outs = pl.pallas_call(
        hand_over,
        out_shape=[jax.ShapeDtypeStruct(o.shape, o.dtype) for o in outs],
        in_specs=[any_space] * 5,
        out_specs=[any_space] * 5,
        scratch_shapes=[pltpu.VMEM(o.shape, o.dtype) for o in outs]
        + [pltpu.SemaphoreType.DMA((5,)), pltpu.SemaphoreType.DMA((5,))],
    )(*outs)
    return (*outs[:4], outs[4].reshape(-1))


def solution(mesh):
    placed = (
        P("dp", "seq", None),
        P("dp", "seq", None),
        P("dp", "seq", None),
        P(),
        P("dp", "seq", None),
    )
    fits = mesh.shape["seq"] == SLOTS and mesh.shape["dp"] == 2
    return jax.shard_map(
        fused_body if fits else body,
        mesh=mesh,
        in_specs=placed,
        out_specs=(
            P("dp", "seq", None),
            P("dp", "seq", None),
            P("dp", "seq", None),
            P("dp", "seq", None),
            P(),
        ),
        check_vma=False,
    )
```
